32 devices in a mesh: ctx: 16 (over z, x, core), head: 2 (over y).
Axes of the slice: x: 2, y: 2, z: 4, core: 2. Of those that a mesh axis runs over, the one named last changes fastest.
Arguments:
- queries: bfloat16 [4096, 4096], P('ctx', 'head'), may hold values from -180 to 180
- keys: bfloat16 [4096, 1024], P('ctx', 'head'), may hold values from -6.5 to 6.5
- values: bfloat16 [4096, 1024], P('ctx', 'head'), may hold values from -6 to 6
- out_grad: bfloat16 [4096, 4096], P('ctx', 'head'), may hold values from -6 to 6
- attn_out: bfloat16 [4096, 4096], P('ctx', 'head'), may hold values from -6 to 6
- lengths: int32 [16], replicated, may hold values from 1 to 1792, as said below
- proj_weight: bfloat16 [4096, 8, 768], P('ctx', 'head'), may hold values from -0.078125 to 0.078125
Outputs:
- input_grad: bfloat16 [4096, 4096], P('ctx', 'head')
The draws below stay inside these ranges and needn't reach their ends.
Inputs may be any that keep to these rules, and one draw needn't show every extreme that they name: `lengths`: every document has 1 to 1792 tokens, one has exactly 1792, and they sum to 4096.
All inputs are finite; a program needn't handle non-finite values.
Results may differ from the reference program's by a relative error of at most 0.013.
Values may be sent and summed in bfloat16 or wider, within the bound.
A program may use at most 192 MiB of HBM per device.

```python
import jax
import jax.numpy as jnp
from jax import lax

D = 4096
HQ = 32
KVH = 8
HD = 128
TOK_DEV = 256
REACH = 7
TOKENS = 4096
DOCS = 16
MAXDOC = 1792
GROUP = 4
N_CTX = 16
N_HEAD = 2


def shared_draw(key):
    query_key = jax.random.fold_in(key, 11)
    keys_key = jax.random.fold_in(key, 12)
    keys = jnp.clip(jax.random.normal(keys_key, (TOKENS, KVH * HD), jnp.float32), -6.0, 6.0)
    queries = jnp.clip(jax.random.normal(query_key, (TOKENS, HQ * HD), jnp.float32), -6.0, 6.0)
    return (queries, keys)


def draw_queries(key, part):
    return shared_draw(key)[0].astype(jnp.bfloat16)


def draw_keys(key, part):
    return shared_draw(key)[1].astype(jnp.bfloat16)


def draw_lengths(key, part):
    jitter_key = jax.random.fold_in(key, 21)
    tail_len = TOK_DEV // 2
    front_total = TOKENS - MAXDOC - tail_len
    front_docs = DOCS - 2
    spacing = front_total // front_docs
    steps = jnp.arange(1, front_docs, dtype=jnp.int32)
    jitter = jax.random.randint(jitter_key, (front_docs - 1,), 0, spacing // 2 + 1, jnp.int32)
    cuts = steps * spacing + jitter
    bounds = jnp.concatenate([jnp.zeros((1,), jnp.int32), cuts, jnp.full((1,), front_total, jnp.int32)])
    front = (bounds[1:] - bounds[:-1]).astype(jnp.int32)
    return jnp.concatenate([front, jnp.full((1,), MAXDOC, jnp.int32), jnp.full((1,), tail_len, jnp.int32)]).astype(jnp.int32)


def block_levels(own_key, extent, split, smallest, largest):
    factor_of, own = 1.0, jax.random.fold_in(own_key, 6)
    for dim, blocks in split:
        steps = jnp.exp(jax.random.uniform(jax.random.fold_in(own, dim), (blocks,), jnp.float32, smallest / len(split), largest / len(split)))
        factor_of = factor_of * jnp.repeat(steps, extent[dim] // blocks).reshape([-1 if axis == dim else 1 for axis in range(len(extent))])
    return factor_of


def scatter_about(key, extent, scale, limit, pieces=(), kind=jnp.bfloat16):
    entries = jax.random.normal(key, extent, jnp.float32) * scale
    if len(pieces) > 0:
        entries = block_levels(key, extent, pieces, -0.22, 0.18) * entries
    return jnp.clip(entries, min=-limit, max=limit).astype(kind)


def setup_inputs(seed: int = 0) -> dict:
    seeds = jax.random.split(jax.random.key(seed), 8)
    return {
        "queries": draw_queries(jax.random.fold_in(seeds[7], 71), 0),
        "keys": draw_keys(jax.random.fold_in(seeds[7], 71), 0),
        "values": scatter_about(seeds[2], (TOKENS, KVH * HD), 1.0, 6.0, ((0, 16), (1, 2))),
        "out_grad": scatter_about(seeds[3], (TOKENS, HQ * HD), 1.0, 6.0, ((0, 16), (1, 2))),
        "attn_out": scatter_about(seeds[4], (TOKENS, HQ * HD), 1.0, 6.0, ((0, 16), (1, 2))),
        "lengths": draw_lengths(jax.random.fold_in(seeds[7], 71), 0),
        "proj_weight": scatter_about(seeds[6], (D, KVH, (GROUP + 2) * HD), ((HQ + 2 * KVH) * HD) ** -0.5, 0.078125, ((0, 16), (1, 2))),
    }


def doc_number(positions, ends):
    counted = jnp.sum((positions[:, None] >= ends[None, :]).astype(jnp.int32), axis=1)
    return jnp.where(positions >= 0, counted, -1).astype(jnp.int32)


def reference(queries, keys, values, out_grad, attn_out, lengths, proj_weight):
    group = HQ // KVH
    window = (REACH + 1) * TOK_DEV
    margin = REACH * TOK_DEV
    scale_factor = HD ** -0.5
    ends = jnp.cumsum(lengths).astype(jnp.int32)
    delta_all = jnp.sum(
        (out_grad.astype(jnp.float32) * attn_out.astype(jnp.float32)).reshape(TOKENS, KVH, group, HD), axis=3)
    key_pad = jnp.concatenate([jnp.zeros((margin, KVH, HD), jnp.float32),
                               keys.astype(jnp.float32).reshape(TOKENS, KVH, HD)], axis=0)
    value_pad = jnp.concatenate([jnp.zeros((margin, KVH, HD), jnp.float32),
                                 values.astype(jnp.float32).reshape(TOKENS, KVH, HD)], axis=0)
    query_all = queries.astype(jnp.float32).reshape(TOKENS, KVH, group, HD)
    dout_all = out_grad.astype(jnp.float32).reshape(TOKENS, KVH, group, HD)

    def one_tile(carry, tile_index):
        key_acc, value_acc = carry
        first = (tile_index * TOK_DEV).astype(jnp.int32)
        query_tile = lax.dynamic_slice_in_dim(query_all, first, TOK_DEV, 0)
        dout_tile = lax.dynamic_slice_in_dim(dout_all, first, TOK_DEV, 0)
        delta_tile = lax.dynamic_slice_in_dim(delta_all, first, TOK_DEV, 0)
        key_tile = lax.dynamic_slice_in_dim(key_pad, first, window, 0)
        value_tile = lax.dynamic_slice_in_dim(value_pad, first, window, 0)
        query_pos = first + jnp.arange(TOK_DEV, dtype=jnp.int32)
        key_pos = first - margin + jnp.arange(window, dtype=jnp.int32)
        allowed = (doc_number(query_pos, ends)[:, None] == doc_number(key_pos, ends)[None, :]) & (
            key_pos[None, :] <= query_pos[:, None])
        scores = jnp.einsum('tkgd,ukd->kgtu', query_tile, key_tile) * scale_factor
        row_max = jnp.max(jnp.where(allowed[None, None], scores, -1e30), axis=3, keepdims=True)
        total = jnp.sum(jnp.where(allowed[None, None], jnp.exp(scores - row_max), 0.0), axis=3, keepdims=True)
        lse_tile = row_max + jnp.log(total)
        probs = jnp.where(allowed[None, None], jnp.exp(scores - lse_tile), 0.0)
        probs_low = lax.optimization_barrier(probs.astype(jnp.bfloat16)).astype(jnp.float32)
        value_grad = jnp.einsum('kgtu,tkgd->ukd', probs_low, dout_tile)
        dprobs = jnp.einsum('tkgd,ukd->kgtu', dout_tile, value_tile)
        delta_here = jnp.transpose(delta_tile, (1, 2, 0))[..., None]
        dscore = (probs * (dprobs - delta_here) * scale_factor).astype(jnp.bfloat16)
        dscore = lax.optimization_barrier(dscore).astype(jnp.float32)
        query_grad = jnp.einsum('kgtu,ukd->tkgd', dscore, key_tile).astype(jnp.bfloat16)
        key_grad = jnp.einsum('kgtu,tkgd->ukd', dscore, query_tile)
        old_keys = lax.dynamic_slice_in_dim(key_acc, first, window, 0)
        old_values = lax.dynamic_slice_in_dim(value_acc, first, window, 0)
        key_acc = lax.dynamic_update_slice_in_dim(key_acc, old_keys + key_grad, first, 0)
        value_acc = lax.dynamic_update_slice_in_dim(value_acc, old_values + value_grad, first, 0)
        return (key_acc, value_acc), query_grad

    start_acc = jnp.zeros((TOKENS + margin, KVH, HD), jnp.float32)
    (key_acc, value_acc), query_tiles = lax.scan(one_tile, (start_acc, start_acc),
                                                 jnp.arange(N_CTX, dtype=jnp.int32))
    query_grad = query_tiles.reshape(TOKENS, KVH, group * HD)
    key_grad = key_acc[margin:].astype(jnp.bfloat16)
    value_grad = value_acc[margin:].astype(jnp.bfloat16)
    combined = jnp.concatenate([query_grad, key_grad, value_grad], axis=2)
    per_block = KVH // N_HEAD
    total = jnp.zeros((TOKENS, D), jnp.float32)
    for block in range(N_HEAD):
        cols = combined[:, block * per_block:(block + 1) * per_block].reshape(TOKENS, -1)
        weights = proj_weight[:, block * per_block:(block + 1) * per_block].reshape(D, -1)
        block_part = lax.dot_general(cols, weights, (((1,), (1,)), ((), ())),
                                     preferred_element_type=jnp.float32).astype(jnp.bfloat16)
        total = total + lax.optimization_barrier(block_part).astype(jnp.float32)
    return total.astype(jnp.bfloat16)
```

```python
import functools
import math

import jax
import jax.numpy as jnp
from jax import lax
from jax.experimental import pallas as pl
from jax.experimental.pallas import tpu as pltpu
from jax.sharding import PartitionSpec as P

HQ = 32
KVH = 8
HD = 128
GROUP = HQ // KVH
QUAD = 4
REACH = 7
NSLOT = 3 * QUAD
MESH = pl.DeviceIdType.MESH
NEG = -1e30


def place(n):
    c = lax.axis_index("ctx")
    m = c // QUAD
    b = (c // 2) % 2
    k = c % 2
    return c, m, b, k, n // QUAD


def greet(n):
    c, m, b, k, quads = place(n)
    barrier = pltpu.get_barrier_semaphore()

    def hello(peer):
        pl.semaphore_signal(barrier, inc=1, device_id={"ctx": peer}, device_id_type=MESH)

    hello(c + 2 - 4 * b)
    hello(c + 1 - 2 * k)

    @pl.when(m > 0)
    def _():
        hello(c - QUAD)

    @pl.when(m < quads - 1)
    def _():
        hello(c + QUAD)

    pl.semaphore_wait(barrier, 2 + jnp.where(m > 0, 1, 0) + jnp.where(m < quads - 1, 1, 0))


def remote(src, dst, send, recv, peer):
    return pltpu.make_async_remote_copy(
        src_ref=src, dst_ref=dst, send_sem=send, recv_sem=recv,
        device_id={"ctx": peer}, device_id_type=MESH)


def gather_kernel(n, kv_ref, out_ref, own_sem, send, recv):
    c, m, b, k, quads = place(n)
    up, other, sib = c + QUAD, c + 2 - 4 * b, c + 1 - 2 * k
    greet(n)

    def slot(dz, bb, kk):
        return out_ref.at[(2 - dz) * QUAD + 2 * bb + kk]

    def has(dz):
        return m >= dz

    def x_from(dz):
        return (b == 0, b >= 0, b == 1)[dz]

    def x_to(dz):
        return (b == 1, b >= 0, b == 0)[dz]

    def z_copy(dz):
        src = kv_ref if dz == 0 else slot(dz, b, k)
        return remote(src, slot(dz + 1, b, k), send.at[dz, 0], recv.at[dz + 1, 0], up)

    def s_copy(dz):
        src = kv_ref if dz == 0 else slot(dz, b, k)
        return remote(src, slot(dz, b, k), send.at[dz, 1], recv.at[dz, 1], sib)

    def x_copy(dz):
        src = kv_ref if dz == 0 else slot(dz, b, k)
        return remote(src, slot(dz, b, k), send.at[dz, 2], recv.at[dz, 2], other)

    def f_copy(dz):
        return remote(slot(dz, 1 - b, k), slot(dz, 1 - b, k), send.at[dz, 3], recv.at[dz, 3], sib)

    own = pltpu.make_async_copy(kv_ref, slot(0, b, k), own_sem)
    own.start()
    for dz in range(3):
        @pl.when(has(dz))
        def _(dz=dz):
            if dz > 0:
                z_copy(dz - 1).wait_recv()
            if dz < 2:
                @pl.when(m < quads - 1)
                def _():
                    z_copy(dz).start()

            @pl.when(x_from(dz))
            def _():
                x_copy(dz).start()
            s_copy(dz).start()

        if dz > 0:
            @pl.when(jnp.logical_and(has(dz - 1), x_to(dz - 1)))
            def _(dz=dz):
                x_copy(dz - 1).wait_recv()
                f_copy(dz - 1).start()

    @pl.when(jnp.logical_and(has(2), x_to(2)))
    def _():
        x_copy(2).wait_recv()
        f_copy(2).start()

    for dz in range(3):
        @pl.when(has(dz))
        def _(dz=dz):
            s_copy(dz).wait_recv()
            s_copy(dz).wait_send()
            if dz < 2:
                @pl.when(m < quads - 1)
                def _():
                    z_copy(dz).wait_send()

            @pl.when(x_from(dz))
            def _():
                x_copy(dz).wait_send()

            @pl.when(x_to(dz))
            def _():
                f_copy(dz).wait_recv()
                f_copy(dz).wait_send()
    own.wait()


def gather_window(n, kv):
    return pl.pallas_call(
        functools.partial(gather_kernel, n),
        out_shape=jax.ShapeDtypeStruct((NSLOT,) + kv.shape, kv.dtype),
        in_specs=[pl.BlockSpec(memory_space=pltpu.VMEM)],
        out_specs=pl.BlockSpec(memory_space=pltpu.VMEM),
        scratch_shapes=[
            pltpu.SemaphoreType.DMA,
            pltpu.SemaphoreType.DMA((3, 4)),
            pltpu.SemaphoreType.DMA((3, 4)),
        ],
        compiler_params=pltpu.CompilerParams(
            collective_id=0, has_side_effects=True, vmem_limit_bytes=32 * 1024 * 1024),
    )(kv)


def reduce_kernel(n, g_ref, out_ref, from_f, from_s, from_x, from_z, sum_x, sum_z, send, recv):
    c, m, b, k, quads = place(n)
    down, other, sib = c - QUAD, c + 2 - 4 * b, c + 1 - 2 * k
    greet(n)

    def part(dz, bb, kk):
        return g_ref.at[(2 - dz) * QUAD + 2 * bb + kk]

    def has(dz):
        return m >= dz

    def x_to(dz):
        return (b == 0, b >= 0, b == 1)[dz]

    def x_from(dz):
        return (b == 1, b >= 0, b == 0)[dz]

    def f_copy(dz):
        return remote(part(dz, 1 - b, 1 - k), from_f.at[dz], send.at[dz, 3], recv.at[dz, 3], sib)

    def s_copy(dz):
        return remote(part(dz, b, 1 - k), from_s.at[dz], send.at[dz, 1], recv.at[dz, 1], sib)

    def x_copy(dz):
        return remote(sum_x.at[dz], from_x.at[dz], send.at[dz, 2], recv.at[dz, 2], other)

    def z_copy(dz):
        return remote(sum_z.at[dz], from_z.at[dz - 1], send.at[dz, 0], recv.at[dz - 1, 0], down)

    for dz in (2, 1, 0):
        @pl.when(has(dz))
        def _(dz=dz):
            @pl.when(x_from(dz))
            def _():
                f_copy(dz).start()
            s_copy(dz).start()

    for dz in (2, 1, 0):
        @pl.when(jnp.logical_and(has(dz), x_from(dz)))
        def _(dz=dz):
            f_copy(dz).wait_recv()
            sum_x[dz] = (part(dz, 1 - b, k)[...].astype(jnp.float32)
                         + from_f[dz].astype(jnp.float32)).astype(sum_x.dtype)
            x_copy(dz).start()

    for dz in (2, 1, 0):
        @pl.when(has(dz))
        def _(dz=dz):
            s_copy(dz).wait_recv()
            sum_z[dz] = (part(dz, b, k)[...].astype(jnp.float32)
                         + from_s[dz].astype(jnp.float32)).astype(sum_z.dtype)

            @pl.when(x_to(dz))
            def _():
                x_copy(dz).wait_recv()
                sum_z[dz] = (sum_z[dz].astype(jnp.float32)
                             + from_x[dz].astype(jnp.float32)).astype(sum_z.dtype)
            if dz < 2:
                @pl.when(m < quads - 1)
                def _():
                    z_copy(dz + 1).wait_recv()
                    sum_z[dz] = (sum_z[dz].astype(jnp.float32)
                                 + from_z[dz].astype(jnp.float32)).astype(sum_z.dtype)
            if dz > 0:
                z_copy(dz).start()

    out_ref[...] = sum_z[0]
    for dz in range(3):
        @pl.when(has(dz))
        def _(dz=dz):
            s_copy(dz).wait_send()

            @pl.when(x_from(dz))
            def _():
                f_copy(dz).wait_send()
                x_copy(dz).wait_send()
            if dz > 0:
                z_copy(dz).wait_send()


def reduce_window(n, parts):
    one = parts.shape[1:]
    vmem = pl.BlockSpec(memory_space=pltpu.VMEM)
    return pl.pallas_call(
        functools.partial(reduce_kernel, n),
        out_shape=jax.ShapeDtypeStruct(one, parts.dtype),
        in_specs=[vmem],
        out_specs=vmem,
        scratch_shapes=[pltpu.VMEM((count,) + one, parts.dtype) for count in (3, 3, 3, 2, 3, 3)] + [
            pltpu.SemaphoreType.DMA((3, 4)),
            pltpu.SemaphoreType.DMA((3, 4)),
        ],
        compiler_params=pltpu.CompilerParams(
            collective_id=1, has_side_effects=True, vmem_limit_bytes=40 * 1024 * 1024),
    )(parts)


def dot(a, b, ca, cb, **kw):
    return lax.dot_general(a, b, (((ca,), (cb,)), ((), ())), preferred_element_type=jnp.float32, **kw)


def attention_kernel(info, q_ref, do_ref, ao_ref, kv_ref, rows_ref, dq_ref, g_ref,
                     qs, dos, s_ref, dqt):
    tile = q_ref.shape[0]
    wide = GROUP * tile
    scale = HD ** (-0.5)
    rate = scale * math.log2(math.e)
    first, own, base = info[0], info[1], info[2]
    prod = do_ref[...].astype(jnp.float32) * ao_ref[...].astype(jnp.float32)
    ones = jnp.ones((8, HD), jnp.float32)
    deltas = []
    for h in range(GROUP):
        cols = slice(h * HD, (h + 1) * HD)
        qs[h * tile:(h + 1) * tile, :] = q_ref[:, cols]
        dos[h * tile:(h + 1) * tile, :] = do_ref[:, cols]
        deltas.append(dot(ones, prod[:, cols], 1, 1, precision=lax.Precision.HIGHEST)[0:1])
    delta = jnp.concatenate(deltas, axis=1)
    start, stop = rows_ref[0:1, :], rows_ref[1:2, :]
    g_ref[...] = jnp.zeros_like(g_ref)
    dqt[...] = jnp.zeros_like(dqt)

    def block(j):
        return pl.ds(pl.multiple_of(j * tile, tile), tile)

    def scan(j, carry):
        top, total = carry
        s = dot(kv_ref[j, 0], qs[...], 1, 1)
        key = base + j * tile + lax.broadcasted_iota(jnp.int32, s.shape, 0)
        s = jnp.where((key >= start) & (key <= stop), s, NEG)
        s_ref[block(j), :] = s
        new = jnp.maximum(top, jnp.max(s, axis=0, keepdims=True))
        here = jnp.sum(jnp.exp2((s - new) * rate), axis=0, keepdims=True)
        return new, total * jnp.exp2((top - new) * rate) + here

    top, total = scan(own, (jnp.full((1, wide), NEG, jnp.float32), jnp.zeros((1, wide), jnp.float32)))
    top, total = lax.fori_loop(first, own, scan, (top, total))
    inverse = 1.0 / total

    def back(j, carry):
        p = jnp.exp2((s_ref[block(j), :] - top) * rate) * inverse
        dp = dot(kv_ref[j, 1], dos[...], 1, 1)
        ds = (p * (dp - delta)).astype(jnp.bfloat16)
        g_ref[j, 1] = dot(p.astype(jnp.bfloat16), dos[...], 1, 0).astype(g_ref.dtype)
        g_ref[j, 0] = (dot(ds, qs[...], 1, 0) * scale).astype(g_ref.dtype)
        dqt[...] += dot(kv_ref[j, 0], ds, 0, 0)
        return carry

    lax.fori_loop(first, own + 1, back, 0)
    dq = jnp.transpose(dqt[...] * scale)
    for h in range(GROUP):
        dq_ref[:, h * HD:(h + 1) * HD] = dq[h * tile:(h + 1) * tile].astype(dq_ref.dtype)


def attention(info, q, do, ao, window, rows):
    tile = q.shape[0]
    groups = q.shape[1] // (GROUP * HD)
    wide = GROUP * tile
    head = pl.BlockSpec((tile, GROUP * HD), lambda g, info: (0, g))
    slots = pl.BlockSpec((NSLOT, 2, tile, HD), lambda g, info: (0, 0, 0, g))
    return pl.pallas_call(
        attention_kernel,
        grid_spec=pltpu.PrefetchScalarGridSpec(
            num_scalar_prefetch=1,
            grid=(groups,),
            in_specs=[head, head, head, slots, pl.BlockSpec((8, wide), lambda g, info: (0, 0))],
            out_specs=[head, slots],
            scratch_shapes=[
                pltpu.VMEM((wide, HD), jnp.bfloat16),
                pltpu.VMEM((wide, HD), jnp.bfloat16),
                pltpu.VMEM((NSLOT * tile, wide), jnp.float32),
                pltpu.VMEM((HD, wide), jnp.float32),
            ],
        ),
        out_shape=[
            jax.ShapeDtypeStruct(q.shape, q.dtype),
            jax.ShapeDtypeStruct(window.shape, window.dtype),
        ],
        compiler_params=pltpu.CompilerParams(vmem_limit_bytes=48 * 1024 * 1024),
        cost_estimate=pl.CostEstimate(
            flops=10 * NSLOT * tile * wide * HD * groups,
            bytes_accessed=4 * window.size + 8 * q.size, transcendentals=0),
    )(info, q, do, ao, window, rows)


def shards(n, queries, keys, values, out_grad, attn_out, lengths, proj_weight):
    tile = queries.shape[0]
    heads_here = keys.shape[1] // HD
    position = lax.axis_index("ctx")
    weights = lax.all_gather(
        proj_weight.reshape(proj_weight.shape[0], -1), "ctx", axis=0, tiled=True)
    window = gather_window(n, jnp.stack([keys, values]))

    ends = jnp.cumsum(lengths)
    query_pos = position * tile + jnp.arange(tile, dtype=jnp.int32)
    start = jnp.max(jnp.where(ends[None, :] <= query_pos[:, None], ends[None, :], 0), axis=1)
    base = (position // QUAD - 2) * QUAD * tile
    own = 2 * QUAD + position % QUAD
    first = jnp.maximum((start[0] - base) // tile, 0)
    info = jnp.stack([first, own, base]).astype(jnp.int32)
    rows = jnp.stack([start, query_pos] + [query_pos] * 6).astype(jnp.int32)
    rows = jnp.tile(rows, (1, GROUP))
    dq, parts = attention(info, queries, out_grad, attn_out, window, rows)
    grads = reduce_window(n, parts)
    combined = jnp.concatenate(
        [dq.reshape(tile, heads_here, GROUP * HD),
         grads[0].reshape(tile, heads_here, HD),
         grads[1].reshape(tile, heads_here, HD)], axis=2).reshape(tile, -1)
    partial_sum = lax.dot_general(
        combined, weights, (((1,), (1,)), ((), ())), preferred_element_type=jnp.float32)
    return lax.psum_scatter(
        partial_sum.astype(jnp.bfloat16), "head", scatter_dimension=1, tiled=True)


def solution(mesh):
    placed = (
        P("ctx", "head"),
        P("ctx", "head"),
        P("ctx", "head"),
        P("ctx", "head"),
        P("ctx", "head"),
        P(),
        P("ctx", "head", None),
    )
    return jax.shard_map(
        functools.partial(shards, mesh.shape["ctx"]),
        mesh=mesh, in_specs=placed, out_specs=P("ctx", "head"), check_vma=False)
```

```python
import functools
import math

import jax
import jax.numpy as jnp
from jax import lax
from jax.experimental import pallas as pl
from jax.experimental.pallas import tpu as pltpu
from jax.sharding import PartitionSpec as P

HQ = 32
KVH = 8
HD = 128
GROUP = HQ // KVH
QUAD = 4
REACH = 7
NSLOT = 3 * QUAD
MESH = pl.DeviceIdType.MESH
NEG = -1e30


def place(n):
    c = lax.axis_index("ctx")
    m = c // QUAD
    b = (c // 2) % 2
    k = c % 2
    return c, m, b, k, n // QUAD


def greet(n):
    c, m, b, k, quads = place(n)
    barrier = pltpu.get_barrier_semaphore()

    def hello(peer):
        pl.semaphore_signal(barrier, inc=1, device_id={"ctx": peer}, device_id_type=MESH)

    hello(c + 2 - 4 * b)
    hello(c + 1 - 2 * k)

    @pl.when(m > 0)
    def _():
        hello(c - QUAD)

    @pl.when(m < quads - 1)
    def _():
        hello(c + QUAD)

    pl.semaphore_wait(barrier, 2 + jnp.where(m > 0, 1, 0) + jnp.where(m < quads - 1, 1, 0))


def remote(src, dst, send, recv, peer):
    return pltpu.make_async_remote_copy(
        src_ref=src, dst_ref=dst, send_sem=send, recv_sem=recv,
        device_id={"ctx": peer}, device_id_type=MESH)


def gather_kernel(n, kv_ref, out_ref, own_sem, send, recv):
    c, m, b, k, quads = place(n)
    up, other, sib = c + QUAD, c + 2 - 4 * b, c + 1 - 2 * k
    greet(n)

    def slot(dz, bb, kk):
        return out_ref.at[(2 - dz) * QUAD + 2 * bb + kk]

    def has(dz):
        return m >= dz

    def x_from(dz):
        return (b == 0, b >= 0, b == 1)[dz]

    def x_to(dz):
        return (b == 1, b >= 0, b == 0)[dz]

    def z_copy(dz):
        src = kv_ref if dz == 0 else slot(dz, b, k)
        return remote(src, slot(dz + 1, b, k), send.at[dz, 0], recv.at[dz + 1, 0], up)

    def s_copy(dz):
        src = kv_ref if dz == 0 else slot(dz, b, k)
        return remote(src, slot(dz, b, k), send.at[dz, 1], recv.at[dz, 1], sib)

    def x_copy(dz):
        src = kv_ref if dz == 0 else slot(dz, b, k)
        return remote(src, slot(dz, b, k), send.at[dz, 2], recv.at[dz, 2], other)

    def f_copy(dz):
        return remote(slot(dz, 1 - b, k), slot(dz, 1 - b, k), send.at[dz, 3], recv.at[dz, 3], sib)

    own = pltpu.make_async_copy(kv_ref, slot(0, b, k), own_sem)
    own.start()
    for dz in range(3):
        @pl.when(has(dz))
        def _(dz=dz):
            if dz > 0:
                z_copy(dz - 1).wait_recv()
            if dz < 2:
                @pl.when(m < quads - 1)
                def _():
                    z_copy(dz).start()

            @pl.when(x_from(dz))
            def _():
                x_copy(dz).start()
            s_copy(dz).start()

        if dz > 0:
            @pl.when(jnp.logical_and(has(dz - 1), x_to(dz - 1)))
            def _(dz=dz):
                x_copy(dz - 1).wait_recv()
                f_copy(dz - 1).start()

    @pl.when(jnp.logical_and(has(2), x_to(2)))
    def _():
        x_copy(2).wait_recv()
        f_copy(2).start()

    for dz in range(3):
        @pl.when(has(dz))
        def _(dz=dz):
            s_copy(dz).wait_recv()
            s_copy(dz).wait_send()
            if dz < 2:
                @pl.when(m < quads - 1)
                def _():
                    z_copy(dz).wait_send()

            @pl.when(x_from(dz))
            def _():
                x_copy(dz).wait_send()

            @pl.when(x_to(dz))
            def _():
                f_copy(dz).wait_recv()
                f_copy(dz).wait_send()
    own.wait()


def gather_window(n, kv):
    return pl.pallas_call(
        functools.partial(gather_kernel, n),
        out_shape=jax.ShapeDtypeStruct((NSLOT,) + kv.shape, kv.dtype),
        in_specs=[pl.BlockSpec(memory_space=pltpu.VMEM)],
        out_specs=pl.BlockSpec(memory_space=pltpu.VMEM),
        scratch_shapes=[
            pltpu.SemaphoreType.DMA,
            pltpu.SemaphoreType.DMA((3, 4)),
            pltpu.SemaphoreType.DMA((3, 4)),
        ],
        compiler_params=pltpu.CompilerParams(
            collective_id=0, has_side_effects=True, vmem_limit_bytes=32 * 1024 * 1024),
    )(kv)


def reduce_kernel(n, g_ref, out_ref, from_f, from_s, from_x, from_z, sum_x, sum_z, send, recv):
    c, m, b, k, quads = place(n)
    down, other, sib = c - QUAD, c + 2 - 4 * b, c + 1 - 2 * k
    greet(n)

    def part(dz, bb, kk):
        return g_ref.at[(2 - dz) * QUAD + 2 * bb + kk]

    def has(dz):
        return m >= dz

    def x_to(dz):
        return (b == 0, b >= 0, b == 1)[dz]

    def x_from(dz):
        return (b == 1, b >= 0, b == 0)[dz]

    def f_copy(dz):
        return remote(part(dz, 1 - b, 1 - k), from_f.at[dz], send.at[dz, 3], recv.at[dz, 3], sib)

    def s_copy(dz):
        return remote(part(dz, b, 1 - k), from_s.at[dz], send.at[dz, 1], recv.at[dz, 1], sib)

    def x_copy(dz):
        return remote(sum_x.at[dz], from_x.at[dz], send.at[dz, 2], recv.at[dz, 2], other)

    def z_copy(dz):
        return remote(sum_z.at[dz], from_z.at[dz - 1], send.at[dz, 0], recv.at[dz - 1, 0], down)

    for dz in (2, 1, 0):
        @pl.when(has(dz))
        def _(dz=dz):
            @pl.when(x_from(dz))
            def _():
                f_copy(dz).start()
            s_copy(dz).start()

    for dz in (2, 1, 0):
        @pl.when(jnp.logical_and(has(dz), x_from(dz)))
        def _(dz=dz):
            f_copy(dz).wait_recv()
            sum_x[dz] = (part(dz, 1 - b, k)[...].astype(jnp.float32)
                         + from_f[dz].astype(jnp.float32)).astype(sum_x.dtype)
            x_copy(dz).start()

    for dz in (2, 1, 0):
        @pl.when(has(dz))
        def _(dz=dz):
            s_copy(dz).wait_recv()
            sum_z[dz] = (part(dz, b, k)[...].astype(jnp.float32)
                         + from_s[dz].astype(jnp.float32)).astype(sum_z.dtype)

            @pl.when(x_to(dz))
            def _():
                x_copy(dz).wait_recv()
                sum_z[dz] = (sum_z[dz].astype(jnp.float32)
                             + from_x[dz].astype(jnp.float32)).astype(sum_z.dtype)
            if dz < 2:
                @pl.when(m < quads - 1)
                def _():
                    z_copy(dz + 1).wait_recv()
                    sum_z[dz] = (sum_z[dz].astype(jnp.float32)
                                 + from_z[dz].astype(jnp.float32)).astype(sum_z.dtype)
            if dz > 0:
                z_copy(dz).start()

    out_ref[...] = sum_z[0]
    for dz in range(3):
        @pl.when(has(dz))
        def _(dz=dz):
            s_copy(dz).wait_send()

            @pl.when(x_from(dz))
            def _():
                f_copy(dz).wait_send()
                x_copy(dz).wait_send()
            if dz > 0:
                z_copy(dz).wait_send()


def reduce_window(n, parts):
    one = parts.shape[1:]
    vmem = pl.BlockSpec(memory_space=pltpu.VMEM)
    return pl.pallas_call(
        functools.partial(reduce_kernel, n),
        out_shape=jax.ShapeDtypeStruct(one, parts.dtype),
        in_specs=[vmem],
        out_specs=vmem,
        scratch_shapes=[pltpu.VMEM((count,) + one, parts.dtype) for count in (3, 3, 3, 2, 3, 3)] + [
            pltpu.SemaphoreType.DMA((3, 4)),
            pltpu.SemaphoreType.DMA((3, 4)),
        ],
        compiler_params=pltpu.CompilerParams(
            collective_id=1, has_side_effects=True, vmem_limit_bytes=40 * 1024 * 1024),
    )(parts)


def dot(a, b, ca, cb, **kw):
    return lax.dot_general(a, b, (((ca,), (cb,)), ((), ())), preferred_element_type=jnp.float32, **kw)


def attention_kernel(info, q_ref, do_ref, ao_ref, kv_ref, rows_ref, dq_ref, g_ref,
                     qs, dos, s_ref, dqt):
    tile = q_ref.shape[0]
    wide = GROUP * tile
    scale = HD ** (-0.5)
    rate = scale * math.log2(math.e)
    first, own, base = info[0], info[1], info[2]
    prod = do_ref[...].astype(jnp.float32) * ao_ref[...].astype(jnp.float32)
    ones = jnp.ones((8, HD), jnp.float32)
    deltas = []
    for h in range(GROUP):
        cols = slice(h * HD, (h + 1) * HD)
        qs[h * tile:(h + 1) * tile, :] = q_ref[:, cols]
        dos[h * tile:(h + 1) * tile, :] = do_ref[:, cols]
        deltas.append(dot(ones, prod[:, cols], 1, 1, precision=lax.Precision.HIGHEST)[0:1])
    delta = jnp.concatenate(deltas, axis=1)
    start, stop = rows_ref[0:1, :], rows_ref[1:2, :]
    g_ref[...] = jnp.zeros_like(g_ref)
    dqt[...] = jnp.zeros_like(dqt)

    def block(j):
        return pl.ds(pl.multiple_of(j * tile, tile), tile)

    def scan(j, carry):
        top, total = carry
        s = dot(kv_ref[j, 0], qs[...], 1, 1)
        key = base + j * tile + lax.broadcasted_iota(jnp.int32, s.shape, 0)
        s = jnp.where((key >= start) & (key <= stop), s, NEG)
        s_ref[block(j), :] = s
        new = jnp.maximum(top, jnp.max(s, axis=0, keepdims=True))
        here = jnp.sum(jnp.exp2((s - new) * rate), axis=0, keepdims=True)
        return new, total * jnp.exp2((top - new) * rate) + here

    top, total = scan(own, (jnp.full((1, wide), NEG, jnp.float32), jnp.zeros((1, wide), jnp.float32)))
    top, total = lax.fori_loop(first, own, scan, (top, total))
    inverse = 1.0 / total

    def back(j, carry):
        p = jnp.exp2((s_ref[block(j), :] - top) * rate) * inverse
        dp = dot(kv_ref[j, 1], dos[...], 1, 1)
        ds = (p * (dp - delta)).astype(jnp.bfloat16)
        g_ref[j, 1] = dot(p.astype(jnp.bfloat16), dos[...], 1, 0).astype(g_ref.dtype)
        g_ref[j, 0] = (dot(ds, qs[...], 1, 0) * scale).astype(g_ref.dtype)
        dqt[...] += dot(kv_ref[j, 0], ds, 0, 0)
        return carry

    lax.fori_loop(first, own + 1, back, 0)
    dq = jnp.transpose(dqt[...] * scale)
    for h in range(GROUP):
        dq_ref[:, h * HD:(h + 1) * HD] = dq[h * tile:(h + 1) * tile].astype(dq_ref.dtype)


def attention(info, q, do, ao, window, rows):
    tile = q.shape[0]
    groups = q.shape[1] // (GROUP * HD)
    wide = GROUP * tile
    head = pl.BlockSpec((tile, GROUP * HD), lambda g, info: (0, g))
    slots = pl.BlockSpec((NSLOT, 2, tile, HD), lambda g, info: (0, 0, 0, g))
    return pl.pallas_call(
        attention_kernel,
        grid_spec=pltpu.PrefetchScalarGridSpec(
            num_scalar_prefetch=1,
            grid=(groups,),
            in_specs=[head, head, head, slots, pl.BlockSpec((8, wide), lambda g, info: (0, 0))],
            out_specs=[head, slots],
            scratch_shapes=[
                pltpu.VMEM((wide, HD), jnp.bfloat16),
                pltpu.VMEM((wide, HD), jnp.bfloat16),
                pltpu.VMEM((NSLOT * tile, wide), jnp.float32),
                pltpu.VMEM((HD, wide), jnp.float32),
            ],
        ),
        out_shape=[
            jax.ShapeDtypeStruct(q.shape, q.dtype),
            jax.ShapeDtypeStruct(window.shape, window.dtype),
        ],
        compiler_params=pltpu.CompilerParams(vmem_limit_bytes=48 * 1024 * 1024),
        cost_estimate=pl.CostEstimate(
            flops=10 * NSLOT * tile * wide * HD * groups,
            bytes_accessed=4 * window.size + 8 * q.size, transcendentals=0),
    )(info, q, do, ao, window, rows)


def project_kernel(heads, dq_ref, g_ref, w_ref, out_ref, rows, came, keep, sent, got, total,
                   c_send, c_recv, y_send, y_recv, o_send, o_recv):
    c = lax.axis_index("ctx")
    y = lax.axis_index("head")
    b, k = (c // 2) % 2, c % 2
    other, sib = c + 2 - 4 * b, c + 1 - 2 * k
    owners = (c, sib, other, other + 1 - 2 * k)
    mine = 2 * b + k
    width = w_ref.shape[0] // heads
    wide = GROUP * HD
    barrier = pltpu.get_barrier_semaphore()
    for peer in owners[1:]:
        pl.semaphore_signal(barrier, inc=1, device_id={"ctx": peer}, device_id_type=MESH)
    for d in range(1, heads):
        pl.semaphore_signal(barrier, inc=1, device_id={"head": lax.rem(y + d, heads)},
                            device_id_type=MESH)
    pl.semaphore_wait(barrier, 3 + heads - 1)

    for g in range(dq_ref.shape[1] // wide):
        at = g * (wide + 2 * HD)
        rows[:, at:at + wide] = dq_ref[:, g * wide:(g + 1) * wide]
        rows[:, at + wide:at + wide + HD] = g_ref[0, :, g * HD:(g + 1) * HD]
        rows[:, at + wide + HD:at + wide + 2 * HD] = g_ref[1, :, g * HD:(g + 1) * HD]

    to_other = remote(rows, came.at[1], c_send.at[1], c_recv.at[1], other)
    to_sib = remote(rows, came.at[0], c_send.at[0], c_recv.at[0], sib)
    onward = remote(came.at[1], came.at[2], c_send.at[2], c_recv.at[2], sib)
    to_other.start()
    to_sib.start()

    def swap(r, d):
        return pltpu.make_async_remote_copy(
            src_ref=sent.at[r, d - 1], dst_ref=got.at[r, d - 1],
            send_sem=y_send.at[r, d - 1], recv_sem=y_recv.at[r, d - 1],
            device_id={"head": lax.rem(y + d, heads)}, device_id_type=MESH)

    def home(r):
        return remote(total.at[r - 1], out_ref.at[mine], o_send.at[r - 1], o_recv.at[r - 1],
                      owners[r])

    def weight(p):
        return w_ref[pl.ds(pl.multiple_of(p * width, width), width), :]

    def finish(r):
        value = keep[r]
        for d in range(1, heads):
            swap(r, d).wait_recv()
            value = value + got[r, d - 1].astype(jnp.float32)
        if r == 0:
            out_ref[mine] = value.astype(out_ref.dtype)
        else:
            total[r - 1] = value.astype(total.dtype)
            home(r).start()

    for r in range(QUAD):
        if r == 1:
            to_sib.wait_recv()
        elif r == 2:
            to_other.wait_recv()
            onward.start()
        elif r == 3:
            onward.wait_recv()
        token_rows = rows if r == 0 else came.at[r - 1]
        for d in range(1, heads):
            sent[r, d - 1] = dot(
                token_rows[...], weight(lax.rem(y + d, heads)), 1, 1).astype(sent.dtype)
            swap(r, d).start()
        keep[r] = dot(token_rows[...], weight(y), 1, 1)
        if r > 0:
            finish(r - 1)
    finish(QUAD - 1)

    to_sib.wait_send()
    to_other.wait_send()
    onward.wait_send()
    for r in range(QUAD):
        for d in range(1, heads):
            swap(r, d).wait_send()
        if r > 0:
            home(r).wait_send()
            home(r).wait_recv()


def project(heads, dq, grads, weights):
    tile = dq.shape[0]
    depth = weights.shape[1]
    width = weights.shape[0] // heads
    low, peers = dq.dtype, max(heads - 1, 1)
    vmem = pl.BlockSpec(memory_space=pltpu.VMEM)
    return pl.pallas_call(
        functools.partial(project_kernel, heads),
        out_shape=jax.ShapeDtypeStruct((QUAD, tile, width), low),
        in_specs=[vmem] * 3,
        out_specs=vmem,
        scratch_shapes=[
            pltpu.VMEM((tile, depth), low),
            pltpu.VMEM((3, tile, depth), low),
            pltpu.VMEM((QUAD, tile, width), jnp.float32),
            pltpu.VMEM((QUAD, peers, tile, width), low),
            pltpu.VMEM((QUAD, peers, tile, width), low),
            pltpu.VMEM((3, tile, width), low),
            pltpu.SemaphoreType.DMA((3,)),
            pltpu.SemaphoreType.DMA((3,)),
            pltpu.SemaphoreType.DMA((QUAD, peers)),
            pltpu.SemaphoreType.DMA((QUAD, peers)),
            pltpu.SemaphoreType.DMA((3,)),
            pltpu.SemaphoreType.DMA((3,)),
        ],
        compiler_params=pltpu.CompilerParams(
            collective_id=2, has_side_effects=True, vmem_limit_bytes=48 * 1024 * 1024),
    )(dq, grads, weights)


def shards(n, heads, queries, keys, values, out_grad, attn_out, lengths, proj_weight):
    tile = queries.shape[0]
    position = lax.axis_index("ctx")
    lines = [list(range(r, n, QUAD)) for r in range(QUAD)]
    weights = lax.all_gather(
        proj_weight.reshape(proj_weight.shape[0], -1), "ctx", axis=0, tiled=True,
        axis_index_groups=lines)
    window = gather_window(n, jnp.stack([keys, values]))

    ends = jnp.cumsum(lengths)
    query_pos = position * tile + jnp.arange(tile, dtype=jnp.int32)
    start = jnp.max(jnp.where(ends[None, :] <= query_pos[:, None], ends[None, :], 0), axis=1)
    base = (position // QUAD - 2) * QUAD * tile
    own = 2 * QUAD + position % QUAD
    first = jnp.maximum((start[0] - base) // tile, 0)
    info = jnp.stack([first, own, base]).astype(jnp.int32)
    rows = jnp.stack([start, query_pos] + [query_pos] * 6).astype(jnp.int32)
    rows = jnp.tile(rows, (1, GROUP))
    dq, parts = attention(info, queries, out_grad, attn_out, window, rows)
    grads = reduce_window(n, parts)
    done = project(heads, dq, grads, weights)
    members, _, width = done.shape
    blocks = weights.shape[0] // proj_weight.shape[0] // heads
    done = done.reshape(members, tile, blocks, width // blocks)
    return jnp.transpose(done, (1, 2, 0, 3)).reshape(tile, members * width)


def solution(mesh):
    placed = (
        P("ctx", "head"),
        P("ctx", "head"),
        P("ctx", "head"),
        P("ctx", "head"),
        P("ctx", "head"),
        P(),
        P("ctx", "head", None),
    )
    return jax.shard_map(
        functools.partial(shards, mesh.shape["ctx"], mesh.shape["head"]),
        mesh=mesh, in_specs=placed, out_specs=P("ctx", "head"), check_vma=False)
```

```python
import functools
import math

import jax
import jax.numpy as jnp
from jax import lax
from jax.experimental import pallas as pl
from jax.experimental.pallas import tpu as pltpu
from jax.sharding import PartitionSpec as P

HQ = 32
KVH = 8
HD = 128
GROUP = HQ // KVH
QUAD = 4
REACH = 7
NSLOT = 3 * QUAD
MESH = pl.DeviceIdType.MESH
NEG = -1e30


def place(n):
    c = lax.axis_index("ctx")
    m = c // QUAD
    b = (c // 2) % 2
    k = c % 2
    return c, m, b, k, n // QUAD


def greet(n):
    c, m, b, k, quads = place(n)
    barrier = pltpu.get_barrier_semaphore()

    def hello(peer):
        pl.semaphore_signal(barrier, inc=1, device_id={"ctx": peer}, device_id_type=MESH)

    hello(c + 2 - 4 * b)
    hello(c + 1 - 2 * k)

    @pl.when(m > 0)
    def _():
        hello(c - QUAD)

    @pl.when(m < quads - 1)
    def _():
        hello(c + QUAD)

    pl.semaphore_wait(barrier, 2 + jnp.where(m > 0, 1, 0) + jnp.where(m < quads - 1, 1, 0))


def remote(src, dst, send, recv, peer):
    return pltpu.make_async_remote_copy(
        src_ref=src, dst_ref=dst, send_sem=send, recv_sem=recv,
        device_id={"ctx": peer}, device_id_type=MESH)


def gather_kernel(n, kv_ref, out_ref, own_sem, send, recv):
    c, m, b, k, quads = place(n)
    up, other, sib = c + QUAD, c + 2 - 4 * b, c + 1 - 2 * k
    greet(n)

    def slot(dz, bb, kk):
        return out_ref.at[(2 - dz) * QUAD + 2 * bb + kk]

    def has(dz):
        return m >= dz

    def x_from(dz):
        return (b == 0, b >= 0, b == 1)[dz]

    def x_to(dz):
        return (b == 1, b >= 0, b == 0)[dz]

    def z_copy(dz):
        src = kv_ref if dz == 0 else slot(dz, b, k)
        return remote(src, slot(dz + 1, b, k), send.at[dz, 0], recv.at[dz + 1, 0], up)

    def s_copy(dz):
        src = kv_ref if dz == 0 else slot(dz, b, k)
        return remote(src, slot(dz, b, k), send.at[dz, 1], recv.at[dz, 1], sib)

    def x_copy(dz):
        src = kv_ref if dz == 0 else slot(dz, b, k)
        return remote(src, slot(dz, b, k), send.at[dz, 2], recv.at[dz, 2], other)

    def f_copy(dz):
        return remote(slot(dz, 1 - b, k), slot(dz, 1 - b, k), send.at[dz, 3], recv.at[dz, 3], sib)

    own = pltpu.make_async_copy(kv_ref, slot(0, b, k), own_sem)
    own.start()
    for dz in range(3):
        @pl.when(has(dz))
        def _(dz=dz):
            if dz > 0:
                z_copy(dz - 1).wait_recv()
            if dz < 2:
                @pl.when(m < quads - 1)
                def _():
                    z_copy(dz).start()

            @pl.when(x_from(dz))
            def _():
                x_copy(dz).start()
            s_copy(dz).start()

        if dz > 0:
            @pl.when(jnp.logical_and(has(dz - 1), x_to(dz - 1)))
            def _(dz=dz):
                x_copy(dz - 1).wait_recv()
                f_copy(dz - 1).start()

    @pl.when(jnp.logical_and(has(2), x_to(2)))
    def _():
        x_copy(2).wait_recv()
        f_copy(2).start()

    for dz in range(3):
        @pl.when(has(dz))
        def _(dz=dz):
            s_copy(dz).wait_recv()
            s_copy(dz).wait_send()
            if dz < 2:
                @pl.when(m < quads - 1)
                def _():
                    z_copy(dz).wait_send()

            @pl.when(x_from(dz))
            def _():
                x_copy(dz).wait_send()

            @pl.when(x_to(dz))
            def _():
                f_copy(dz).wait_recv()
                f_copy(dz).wait_send()
    own.wait()


def gather_window(n, kv):
    return pl.pallas_call(
        functools.partial(gather_kernel, n),
        out_shape=jax.ShapeDtypeStruct((NSLOT,) + kv.shape, kv.dtype),
        in_specs=[pl.BlockSpec(memory_space=pltpu.VMEM)],
        out_specs=pl.BlockSpec(memory_space=pltpu.VMEM),
        scratch_shapes=[
            pltpu.SemaphoreType.DMA,
            pltpu.SemaphoreType.DMA((3, 4)),
            pltpu.SemaphoreType.DMA((3, 4)),
        ],
        compiler_params=pltpu.CompilerParams(
            collective_id=0, has_side_effects=True, vmem_limit_bytes=32 * 1024 * 1024),
    )(kv)


def reduce_kernel(n, g_ref, dq_ref, out_ref, came, from_f, from_s, from_x, from_z, sum_x, sum_z,
                  send, recv, q_send, q_recv):
    c, m, b, k, quads = place(n)
    down, other, sib = c - QUAD, c + 2 - 4 * b, c + 1 - 2 * k
    greet(n)

    def part(dz, bb, kk):
        return g_ref.at[(2 - dz) * QUAD + 2 * bb + kk]

    def has(dz):
        return m >= dz

    def x_to(dz):
        return (b == 0, b >= 0, b == 1)[dz]

    def x_from(dz):
        return (b == 1, b >= 0, b == 0)[dz]

    def f_copy(dz):
        return remote(part(dz, 1 - b, 1 - k), from_f.at[dz], send.at[dz, 3], recv.at[dz, 3], sib)

    def s_copy(dz):
        return remote(part(dz, b, 1 - k), from_s.at[dz], send.at[dz, 1], recv.at[dz, 1], sib)

    def x_copy(dz):
        return remote(sum_x.at[dz], from_x.at[dz], send.at[dz, 2], recv.at[dz, 2], other)

    def z_copy(dz):
        return remote(sum_z.at[dz], from_z.at[dz - 1], send.at[dz, 0], recv.at[dz - 1, 0], down)

    to_sib = remote(dq_ref, came.at[0], q_send.at[0], q_recv.at[0], sib)
    to_other = remote(dq_ref, came.at[1], q_send.at[1], q_recv.at[1], other)
    onward = remote(came.at[1], came.at[2], q_send.at[2], q_recv.at[2], sib)

    for dz in (2, 1, 0):
        @pl.when(has(dz))
        def _(dz=dz):
            @pl.when(x_from(dz))
            def _():
                f_copy(dz).start()
            s_copy(dz).start()

    for dz in (2, 1, 0):
        @pl.when(jnp.logical_and(has(dz), x_from(dz)))
        def _(dz=dz):
            f_copy(dz).wait_recv()
            sum_x[dz] = (part(dz, 1 - b, k)[...].astype(jnp.float32)
                         + from_f[dz].astype(jnp.float32)).astype(sum_x.dtype)
            x_copy(dz).start()

    to_other.start()
    to_sib.start()
    for dz in (2, 1, 0):
        @pl.when(has(dz))
        def _(dz=dz):
            s_copy(dz).wait_recv()
            sum_z[dz] = (part(dz, b, k)[...].astype(jnp.float32)
                         + from_s[dz].astype(jnp.float32)).astype(sum_z.dtype)

            @pl.when(x_to(dz))
            def _():
                x_copy(dz).wait_recv()
                sum_z[dz] = (sum_z[dz].astype(jnp.float32)
                             + from_x[dz].astype(jnp.float32)).astype(sum_z.dtype)
            if dz < 2:
                @pl.when(m < quads - 1)
                def _():
                    z_copy(dz + 1).wait_recv()
                    sum_z[dz] = (sum_z[dz].astype(jnp.float32)
                                 + from_z[dz].astype(jnp.float32)).astype(sum_z.dtype)
            if dz > 0:
                z_copy(dz).start()

    out_ref[...] = sum_z[0]
    to_other.wait_recv()
    onward.start()
    to_sib.wait()
    to_other.wait_send()
    onward.wait()
    for dz in range(3):
        @pl.when(has(dz))
        def _(dz=dz):
            s_copy(dz).wait_send()

            @pl.when(x_from(dz))
            def _():
                f_copy(dz).wait_send()
                x_copy(dz).wait_send()
            if dz > 0:
                z_copy(dz).wait_send()


def reduce_window(n, parts, dq):
    one = parts.shape[1:]
    vmem = pl.BlockSpec(memory_space=pltpu.VMEM)
    return pl.pallas_call(
        functools.partial(reduce_kernel, n),
        out_shape=[jax.ShapeDtypeStruct(one, parts.dtype),
                   jax.ShapeDtypeStruct((3,) + dq.shape, dq.dtype)],
        in_specs=[vmem, vmem],
        out_specs=[vmem, vmem],
        scratch_shapes=[pltpu.VMEM((count,) + one, parts.dtype) for count in (3, 3, 3, 2, 3, 3)] + [
            pltpu.SemaphoreType.DMA((3, 4)),
            pltpu.SemaphoreType.DMA((3, 4)),
            pltpu.SemaphoreType.DMA((3,)),
            pltpu.SemaphoreType.DMA((3,)),
        ],
        compiler_params=pltpu.CompilerParams(
            collective_id=1, has_side_effects=True, vmem_limit_bytes=40 * 1024 * 1024),
    )(parts, dq)


def dot(a, b, ca, cb, **kw):
    return lax.dot_general(a, b, (((ca,), (cb,)), ((), ())), preferred_element_type=jnp.float32, **kw)


def attention_kernel(info, q_ref, do_ref, ao_ref, kv_ref, rows_ref, dq_ref, g_ref,
                     qs, dos, s_ref, dqt):
    tile = q_ref.shape[0]
    wide = GROUP * tile
    scale = HD ** (-0.5)
    rate = scale * math.log2(math.e)
    first, own, base = info[0], info[1], info[2]
    prod = do_ref[...].astype(jnp.float32) * ao_ref[...].astype(jnp.float32)
    ones = jnp.ones((8, HD), jnp.float32)
    deltas = []
    for h in range(GROUP):
        cols = slice(h * HD, (h + 1) * HD)
        qs[h * tile:(h + 1) * tile, :] = q_ref[:, cols]
        dos[h * tile:(h + 1) * tile, :] = do_ref[:, cols]
        deltas.append(dot(ones, prod[:, cols], 1, 1, precision=lax.Precision.HIGHEST)[0:1])
    delta = jnp.concatenate(deltas, axis=1)
    start, stop = rows_ref[0:1, :], rows_ref[1:2, :]
    g_ref[...] = jnp.zeros_like(g_ref)
    dqt[...] = jnp.zeros_like(dqt)

    def block(j):
        return pl.ds(pl.multiple_of(j * tile, tile), tile)

    def scan(j, carry):
        top, total = carry
        s = dot(kv_ref[j, 0], qs[...], 1, 1)
        key = base + j * tile + lax.broadcasted_iota(jnp.int32, s.shape, 0)
        s = jnp.where((key >= start) & (key <= stop), s, NEG)
        s_ref[block(j), :] = s
        new = jnp.maximum(top, jnp.max(s, axis=0, keepdims=True))
        here = jnp.sum(jnp.exp2((s - new) * rate), axis=0, keepdims=True)
        return new, total * jnp.exp2((top - new) * rate) + here

    top, total = scan(own, (jnp.full((1, wide), NEG, jnp.float32), jnp.zeros((1, wide), jnp.float32)))
    top, total = lax.fori_loop(first, own, scan, (top, total))
    inverse = 1.0 / total

    def back(j, carry):
        p = jnp.exp2((s_ref[block(j), :] - top) * rate) * inverse
        dp = dot(kv_ref[j, 1], dos[...], 1, 1)
        ds = (p * (dp - delta)).astype(jnp.bfloat16)
        g_ref[j, 1] = dot(p.astype(jnp.bfloat16), dos[...], 1, 0).astype(g_ref.dtype)
        g_ref[j, 0] = (dot(ds, qs[...], 1, 0) * scale).astype(g_ref.dtype)
        dqt[...] += dot(kv_ref[j, 0], ds, 0, 0)
        return carry

    lax.fori_loop(first, own + 1, back, 0)
    dq = jnp.transpose(dqt[...] * scale)
    for h in range(GROUP):
        dq_ref[:, h * HD:(h + 1) * HD] = dq[h * tile:(h + 1) * tile].astype(dq_ref.dtype)


def attention(info, q, do, ao, window, rows):
    tile = q.shape[0]
    groups = q.shape[1] // (GROUP * HD)
    wide = GROUP * tile
    head = pl.BlockSpec((tile, GROUP * HD), lambda g, info: (0, g))
    slots = pl.BlockSpec((NSLOT, 2, tile, HD), lambda g, info: (0, 0, 0, g))
    return pl.pallas_call(
        attention_kernel,
        grid_spec=pltpu.PrefetchScalarGridSpec(
            num_scalar_prefetch=1,
            grid=(groups,),
            in_specs=[head, head, head, slots, pl.BlockSpec((8, wide), lambda g, info: (0, 0))],
            out_specs=[head, slots],
            scratch_shapes=[
                pltpu.VMEM((wide, HD), jnp.bfloat16),
                pltpu.VMEM((wide, HD), jnp.bfloat16),
                pltpu.VMEM((NSLOT * tile, wide), jnp.float32),
                pltpu.VMEM((HD, wide), jnp.float32),
            ],
        ),
        out_shape=[
            jax.ShapeDtypeStruct(q.shape, q.dtype),
            jax.ShapeDtypeStruct(window.shape, window.dtype),
        ],
        compiler_params=pltpu.CompilerParams(vmem_limit_bytes=48 * 1024 * 1024),
        cost_estimate=pl.CostEstimate(
            flops=10 * NSLOT * tile * wide * HD * groups,
            bytes_accessed=4 * window.size + 8 * q.size, transcendentals=0),
    )(info, q, do, ao, window, rows)


def project_kernel(heads, dq_ref, quad_ref, g_ref, w_ref, out_ref, rows, came, keep, sent, got, total,
                   c_send, c_recv, y_send, y_recv, o_send, o_recv):
    c = lax.axis_index("ctx")
    y = lax.axis_index("head")
    b, k = (c // 2) % 2, c % 2
    other, sib = c + 2 - 4 * b, c + 1 - 2 * k
    owners = (c, sib, other, other + 1 - 2 * k)
    mine = 2 * b + k
    width = w_ref.shape[0] // heads
    wide = GROUP * HD
    barrier = pltpu.get_barrier_semaphore()
    for peer in owners[1:]:
        pl.semaphore_signal(barrier, inc=1, device_id={"ctx": peer}, device_id_type=MESH)
    for d in range(1, heads):
        pl.semaphore_signal(barrier, inc=1, device_id={"head": lax.rem(y + d, heads)},
                            device_id_type=MESH)
    pl.semaphore_wait(barrier, 3 + heads - 1)

    def assemble(r):
        heads_of, pair = (dq_ref, g_ref) if r == 0 else (quad_ref.at[r - 1], came.at[r - 1])
        for g in range(dq_ref.shape[1] // wide):
            at = g * (wide + 2 * HD)
            rows[r, :, at:at + wide] = heads_of[:, g * wide:(g + 1) * wide]
            rows[r, :, at + wide:at + wide + HD] = pair[0, :, g * HD:(g + 1) * HD]
            rows[r, :, at + wide + HD:at + wide + 2 * HD] = pair[1, :, g * HD:(g + 1) * HD]

    to_other = remote(g_ref, came.at[1], c_send.at[1], c_recv.at[1], other)
    to_sib = remote(g_ref, came.at[0], c_send.at[0], c_recv.at[0], sib)
    onward = remote(came.at[1], came.at[2], c_send.at[2], c_recv.at[2], sib)
    to_other.start()
    to_sib.start()

    def swap(r, d):
        return pltpu.make_async_remote_copy(
            src_ref=sent.at[r, d - 1], dst_ref=got.at[r, d - 1],
            send_sem=y_send.at[r, d - 1], recv_sem=y_recv.at[r, d - 1],
            device_id={"head": lax.rem(y + d, heads)}, device_id_type=MESH)

    def home(r):
        return remote(total.at[r - 1], out_ref.at[mine], o_send.at[r - 1], o_recv.at[r - 1],
                      owners[r])

    def weight(p):
        return w_ref[pl.ds(pl.multiple_of(p * width, width), width), :]

    def finish(r):
        value = keep[r]
        for d in range(1, heads):
            swap(r, d).wait_recv()
            value = value + got[r, d - 1].astype(jnp.float32)
        if r == 0:
            out_ref[mine] = value.astype(out_ref.dtype)
        else:
            total[r - 1] = value.astype(total.dtype)
            home(r).start()

    for r in range(QUAD):
        if r == 1:
            to_sib.wait_recv()
        elif r == 2:
            to_other.wait_recv()
            onward.start()
        elif r == 3:
            onward.wait_recv()
        assemble(r)
        for d in range(1, heads):
            sent[r, d - 1] = dot(
                rows[r], weight(lax.rem(y + d, heads)), 1, 1).astype(sent.dtype)
            swap(r, d).start()
        keep[r] = dot(rows[r], weight(y), 1, 1)
        if r > 0:
            finish(r - 1)
    finish(QUAD - 1)

    to_sib.wait_send()
    to_other.wait_send()
    onward.wait_send()
    for r in range(QUAD):
        for d in range(1, heads):
            swap(r, d).wait_send()
        if r > 0:
            home(r).wait_send()
            home(r).wait_recv()


def project(heads, dq, dq_quad, grads, weights):
    tile = dq.shape[0]
    depth = weights.shape[1]
    width = weights.shape[0] // heads
    low, peers = dq.dtype, max(heads - 1, 1)
    vmem = pl.BlockSpec(memory_space=pltpu.VMEM)
    return pl.pallas_call(
        functools.partial(project_kernel, heads),
        out_shape=jax.ShapeDtypeStruct((QUAD, tile, width), low),
        in_specs=[vmem] * 4,
        out_specs=vmem,
        scratch_shapes=[
            pltpu.VMEM((QUAD, tile, depth), low),
            pltpu.VMEM((3,) + grads.shape, low),
            pltpu.VMEM((QUAD, tile, width), jnp.float32),
            pltpu.VMEM((QUAD, peers, tile, width), low),
            pltpu.VMEM((QUAD, peers, tile, width), low),
            pltpu.VMEM((3, tile, width), low),
            pltpu.SemaphoreType.DMA((3,)),
            pltpu.SemaphoreType.DMA((3,)),
            pltpu.SemaphoreType.DMA((QUAD, peers)),
            pltpu.SemaphoreType.DMA((QUAD, peers)),
            pltpu.SemaphoreType.DMA((3,)),
            pltpu.SemaphoreType.DMA((3,)),
        ],
        compiler_params=pltpu.CompilerParams(
            collective_id=2, has_side_effects=True, vmem_limit_bytes=48 * 1024 * 1024),
    )(dq, dq_quad, grads, weights)


def shards(n, heads, queries, keys, values, out_grad, attn_out, lengths, proj_weight):
    tile = queries.shape[0]
    position = lax.axis_index("ctx")
    window = gather_window(n, jnp.stack([keys, values]))
    lines = [list(range(r, n, QUAD)) for r in range(QUAD)]
    window, held = lax.optimization_barrier(
        (window, proj_weight.reshape(proj_weight.shape[0], -1)))
    weights = lax.all_gather(held, "ctx", axis=0, tiled=True, axis_index_groups=lines)

    ends = jnp.cumsum(lengths)
    query_pos = position * tile + jnp.arange(tile, dtype=jnp.int32)
    start = jnp.max(jnp.where(ends[None, :] <= query_pos[:, None], ends[None, :], 0), axis=1)
    base = (position // QUAD - 2) * QUAD * tile
    own = 2 * QUAD + position % QUAD
    first = jnp.maximum((start[0] - base) // tile, 0)
    info = jnp.stack([first, own, base]).astype(jnp.int32)
    rows = jnp.stack([start, query_pos] + [query_pos] * 6).astype(jnp.int32)
    rows = jnp.tile(rows, (1, GROUP))
    dq, parts = attention(info, queries, out_grad, attn_out, window, rows)
    grads, dq_quad = reduce_window(n, parts, dq)
    done = project(heads, dq, dq_quad, grads, weights)
    members, _, width = done.shape
    blocks = weights.shape[0] // proj_weight.shape[0] // heads
    done = done.reshape(members, tile, blocks, width // blocks)
    return jnp.transpose(done, (1, 2, 0, 3)).reshape(tile, members * width)


def solution(mesh):
    placed = (
        P("ctx", "head"),
        P("ctx", "head"),
        P("ctx", "head"),
        P("ctx", "head"),
        P("ctx", "head"),
        P(),
        P("ctx", "head", None),
    )
    return jax.shard_map(
        functools.partial(shards, mesh.shape["ctx"], mesh.shape["head"]),
        mesh=mesh, in_specs=placed, out_specs=P("ctx", "head"), check_vma=False)
```
